32 devices in a mesh: event: 16 (over z, x, core), wrow: 2 (over y).
Axes of the slice: x: 2, y: 2, z: 4, core: 2. Of those that a mesh axis runs over, the one named last changes fastest.
Arguments:
- mc_mass: float32 [49152], P('event'), may hold values from 0.5 to 4
- mc_basis: bfloat16 [64, 49152], P(None, 'event'), may hold values from -4 to 4
- data_mass: float32 [65536], P('event'), may hold values from 0.5 to 4
- data_basis: bfloat16 [64, 65536], P(None, 'event'), may hold values from -4 to 4
- data_weight: float32 [65536], P('event'), may hold values from 0.2 to 7.2, as said below
- res_mass: float32 [1024], P('wrow'), may hold values from 0.8 to 1.9
- res_width: float32 [1024], P('wrow'), may hold values from 0.05 to 0.5
- res_wave: int32 [1024], P('wrow'), may hold values from 0 to 511, as said below
- wave_q: int32 [512], P('wrow'), may hold values from 0 to 63
- couplings: float32 [2, 512], P(None, 'wrow'), may hold values from -0.25 to 0.25
Outputs:
- coupling_out: float32 [2, 512], P(None, 'wrow')
- intensity: float32 [65536], P('event')
The draws below stay inside these ranges and needn't reach their ends.
Inputs may be any that keep to these rules, and one draw needn't show every extreme that they name: Resonance r belongs to a wave of block r // 512: res_wave[r] // 256 == r // 512; every wave has exactly 2 resonances. `data_weight`: positive event weights.
All inputs are finite; a program needn't handle non-finite values.
Results may differ from the reference program's by a relative error of at most 0.0024.
Values may be sent and summed in bfloat16 or wider, within the bound.
A program may use at most 64 MiB of HBM per device.

```python
import math
import jax
import jax.numpy as jnp
from jax import lax

W = 512
Q = 64
MC_DEV = 3072
DATA_DEV = 4096
ITERS = 3
RES = 1024
WAVE_DEV = 256
RES_DEV = 512
EVENTS_MC = 49152
EVENTS_DATA = 65536
N_EVENT = 16


def draw_res_wave(key, part):
    blocks = RES // RES_DEV
    subkeys = jax.random.split(key, blocks)
    pattern = jnp.arange(RES_DEV, dtype=jnp.int32) % WAVE_DEV
    local_wave = jax.vmap(lambda subkey: jax.random.permutation(subkey, pattern))(subkeys)
    offsets = (jnp.arange(blocks, dtype=jnp.int32) * WAVE_DEV)[:, None]
    return (local_wave + offsets).reshape(RES)


def draw_data_weight(key, part):
    position = jnp.arange(EVENTS_DATA, dtype=jnp.float32) / EVENTS_DATA
    spread = jax.random.uniform(key, (EVENTS_DATA,), jnp.float32, 0.5, 1.5)
    ramp = 1.0 + 2.0 * position
    return spread * ramp


def set_ends(drawn, key, smallest, top_value):
    shape = drawn.shape
    index_at = [jax.random.randint(jax.random.fold_in(key, axis), (), 0, shape[axis]) for axis in range(len(shape))]
    drawn = drawn.at[tuple(index_at)].set(smallest)
    longest = shape.index(max(shape))
    index_at[longest] = (index_at[longest] + 1) % shape[longest]
    return drawn.at[tuple(index_at)].set(top_value)


def level_of(own_key, shape, cuts, smallest, high):
    loudness = 1.0
    for dim, blocks in cuts:
        draws = jax.random.uniform(jax.random.fold_in(jax.random.fold_in(own_key, 6), dim), (blocks,), jnp.float32, smallest / len(cuts), high / len(cuts))
        loudness = loudness * jnp.repeat(jnp.exp(draws), shape[dim] // blocks).reshape((-1,) + (1,) * (len(shape) - 1 - dim))
    return loudness


def gaussian(own_key, extent, deviation, bound, pieces=(), kind=jnp.bfloat16):
    array = deviation * jax.random.normal(own_key, extent, jnp.float32)
    if pieces:
        array = array * level_of(own_key, extent, pieces, -0.22, 0.18)
    return jnp.clip(array, -bound, bound).astype(kind)


def setup_inputs(seed: int = 0) -> dict:
    key_of = jax.random.split(jax.random.key(seed), 11)
    return {
        "mc_mass": jnp.clip(0.5 + 3.5 * jax.random.uniform(key_of[0], (EVENTS_MC,), jnp.float32) ** level_of(key_of[0], (EVENTS_MC,), ((0, 16),), -0.2, 0.2), 0.5, 4.0),
        "mc_basis": gaussian(key_of[1], (Q, EVENTS_MC), 1.0, 4.0, ((1, 16),)),
        "data_mass": jnp.clip(0.5 + 3.5 * jax.random.uniform(key_of[2], (EVENTS_DATA,), jnp.float32) ** level_of(key_of[2], (EVENTS_DATA,), ((0, 16),), -0.2, 0.2), 0.5, 4.0),
        "data_basis": gaussian(key_of[3], (Q, EVENTS_DATA), 1.0, 4.0, ((1, 16),)),
        "data_weight": draw_data_weight(jax.random.fold_in(key_of[10], 71), 0),
        "res_mass": jnp.clip(0.8 + 1.09999996 * jax.random.uniform(key_of[5], (RES,), jnp.float32) ** level_of(key_of[5], (RES,), ((0, 2),), -0.2, 0.2), 0.8, 1.9),
        "res_width": jnp.clip(jnp.exp(math.log(0.5) - 2.3025851 * jax.random.uniform(key_of[6], (RES,), jnp.float32) ** level_of(key_of[6], (RES,), ((0, 2),), -0.2, 0.2)), 0.05, 0.5),
        "res_wave": draw_res_wave(jax.random.fold_in(key_of[10], 71), 0),
        "wave_q": set_ends(jax.random.randint(key_of[8], (W,), 0, Q), jax.random.fold_in(key_of[8], 1), 0, Q - 1).astype(jnp.int32),
        "couplings": gaussian(key_of[9], (2, W), W ** -0.5, 0.25, ((1, 2),), jnp.float32),
    }


BACKGROUND = 0.5


def amplitudes(mass_sq, angular_basis, res_mass, res_width, res_wave, wave_q):
    product = res_mass * res_width
    spacing = (res_mass * res_mass)[:, None] - mass_sq[None, :]
    denominator = spacing * spacing + (product * product)[:, None]
    real_part = product[:, None] * spacing / denominator
    imag_part = (product * product)[:, None] / denominator
    summed_real = jax.ops.segment_sum(real_part, res_wave, num_segments=W)
    summed_imag = jax.ops.segment_sum(imag_part, res_wave, num_segments=W)
    angular = angular_basis[wave_q, :].astype(jnp.float32)
    return jnp.concatenate([angular * summed_real, angular * summed_imag], axis=0).astype(jnp.bfloat16)


def reference(mc_mass, mc_basis, data_mass, data_basis, data_weight, res_mass, res_width, res_wave, wave_q, couplings):
    highest = lax.Precision.HIGHEST
    mc_blocks = (mc_mass.reshape(N_EVENT, MC_DEV), mc_basis.reshape(Q, N_EVENT, MC_DEV).transpose(1, 0, 2))

    def gram_step(running, block):
        stacked = amplitudes(block[0], block[1], res_mass, res_width, res_wave, wave_q)
        products = lax.dot_general(stacked, stacked, (((1,), (1,)), ((), ())), preferred_element_type=jnp.float32)
        return running + products, None

    products, unused = lax.scan(gram_step, jnp.zeros((2 * W, 2 * W), jnp.float32), mc_blocks)
    normalize = 1.0 / EVENTS_MC
    gram_real = (products[:W, :W] + products[W:, W:]) * normalize
    gram_imag = (products[:W, W:] - products[W:, :W]) * normalize
    row_weight = jnp.sum(jnp.abs(gram_real) + jnp.abs(gram_imag), axis=1)
    data_blocks = (data_mass.reshape(N_EVENT, DATA_DEV), data_basis.reshape(Q, N_EVENT, DATA_DEV).transpose(1, 0, 2), data_weight.reshape(N_EVENT, DATA_DEV))
    inverse_count = 1.0 / EVENTS_DATA

    def data_pass(coupling):
        kernel = jnp.stack([jnp.concatenate([coupling[0], -coupling[1]]), jnp.concatenate([coupling[1], coupling[0]])])

        def data_step(running, block):
            stacked = amplitudes(block[0], block[1], res_mass, res_width, res_wave, wave_q)
            field_sum = jnp.dot(kernel, stacked, preferred_element_type=jnp.float32, precision=highest)
            power = field_sum[0] * field_sum[0] + field_sum[1] * field_sum[1]
            intensity = power + BACKGROUND
            weighting = block[2] / intensity
            carried = jnp.stack([field_sum[0] * weighting, field_sum[1] * weighting], axis=1)
            projected = jnp.dot(stacked, carried, preferred_element_type=jnp.float32, precision=highest)
            real_amp = stacked[:W].astype(jnp.float32)
            imag_amp = stacked[W:].astype(jnp.float32)
            squares = real_amp * real_amp + imag_amp * imag_amp
            curvature = jnp.dot(squares, block[2] * power / (intensity * intensity), precision=highest)
            return (running[0] + projected, running[1] + curvature), intensity

        start = (jnp.zeros((2 * W, 2), jnp.float32), jnp.zeros((W,), jnp.float32))
        return lax.scan(data_step, start, data_blocks)

    coupling = couplings
    for iteration in range(ITERS):
        (projected, curvature), unused = data_pass(coupling)
        mixed_real = jnp.dot(gram_real, coupling[0], precision=highest) - jnp.dot(gram_imag, coupling[1], precision=highest)
        mixed_imag = jnp.dot(gram_real, coupling[1], precision=highest) + jnp.dot(gram_imag, coupling[0], precision=highest)
        grad_real = -(projected[:W, 0] + projected[W:, 1]) * inverse_count + mixed_real
        grad_imag = -(projected[:W, 1] - projected[W:, 0]) * inverse_count + mixed_imag
        total_curve = curvature * inverse_count + row_weight
        coupling = coupling - jnp.stack([grad_real, grad_imag]) / total_curve[None, :]
    unused, intensity = data_pass(coupling)
    return coupling, intensity.reshape(EVENTS_DATA)
```

```python
import jax
import jax.numpy as jnp
from jax import lax
from jax.sharding import PartitionSpec as P

ITERS = 3
BACKGROUND = 0.5


def split_two(value):
    high = lax.reduce_precision(value, 8, 7)
    return high.astype(jnp.bfloat16), (value - high).astype(jnp.bfloat16)


def wave_table(res_mass, res_width, local_wave, wave_q):
    waves = jnp.arange(wave_q.shape[0], dtype=jnp.int32)[:, None]
    index = jnp.arange(res_mass.shape[0], dtype=jnp.int32)[None, :]
    mine = local_wave[None, :] == waves
    first = jnp.min(jnp.where(mine, index, res_mass.shape[0]), axis=1, keepdims=True)
    last = jnp.max(jnp.where(mine, index, -1), axis=1, keepdims=True)

    def pick(where, values):
        return jnp.sum(jnp.where(index == where, values[None, :], 0.0), axis=1)

    return jnp.stack(
        [
            pick(first, res_mass),
            pick(first, res_width),
            pick(last, res_mass),
            pick(last, res_width),
            wave_q.astype(jnp.float32),
        ]
    )


def wave_amplitudes(mass_sq, angular_basis, table):
    def shape_of(mass, width):
        product = (mass * width)[:, None]
        spacing = (mass * mass)[:, None] - mass_sq[None, :]
        scale = product / (spacing * spacing + product * product)
        return scale * spacing, scale * product

    real_a, imag_a = shape_of(table[0], table[1])
    real_b, imag_b = shape_of(table[2], table[3])
    levels = jnp.arange(angular_basis.shape[0], dtype=jnp.float32)
    chooser = (table[4][:, None] == levels[None, :]).astype(jnp.bfloat16)
    angular = jnp.dot(chooser, angular_basis, preferred_element_type=jnp.float32)
    return (
        (angular * (real_a + real_b)).astype(jnp.bfloat16),
        (angular * (imag_a + imag_b)).astype(jnp.bfloat16),
    )


def dot_last(left, right):
    return lax.dot_general(
        left, right, (((1,), (1,)), ((), ())), preferred_element_type=jnp.float32
    )


def shards(
    mc_mass,
    mc_basis,
    data_mass,
    data_basis,
    data_weight,
    res_mass,
    res_width,
    res_wave,
    wave_q,
    couplings,
):
    highest = lax.Precision.HIGHEST
    wave_count = wave_q.shape[0]
    event_devices = lax.axis_size("event")
    row_devices = lax.axis_size("wrow")
    row_index = lax.axis_index("wrow")
    local = wave_table(res_mass, res_width, res_wave - row_index * wave_count, wave_q)
    gathered = lax.all_gather(
        jnp.concatenate([local, couplings], axis=0), "wrow", axis=1, tiled=True
    )
    table, coupling = gathered[:5], gathered[5:7]
    waves = gathered.shape[1]
    mine = row_index * wave_count

    mc_real, mc_imag = wave_amplitudes(mc_mass, mc_basis, table)
    left = jnp.concatenate(
        [
            lax.dynamic_slice_in_dim(mc_real, mine, wave_count),
            lax.dynamic_slice_in_dim(mc_imag, mine, wave_count),
        ],
        axis=0,
    )
    by_real = dot_last(left, mc_real)
    by_imag = dot_last(left, mc_imag)
    normalize = 1.0 / (mc_mass.shape[0] * event_devices)
    gram_part = jnp.concatenate(
        [
            (by_real[:wave_count] + by_imag[wave_count:]) * normalize,
            (by_imag[:wave_count] - by_real[wave_count:]) * normalize,
        ],
        axis=1,
    )
    gram = lax.psum_scatter(gram_part, "event", scatter_dimension=0, tiled=True)
    gram_rows = gram.shape[0]
    gram_at = mine + lax.axis_index("event") * gram_rows

    share = data_mass.shape[0] // row_devices
    start = row_index * share
    mass_here = lax.dynamic_slice_in_dim(data_mass, start, share)
    basis_here = lax.dynamic_slice_in_dim(data_basis, start, share, axis=1)
    weight_here = lax.dynamic_slice_in_dim(data_weight, start, share)
    data_real, data_imag = wave_amplitudes(mass_here, basis_here, table)
    real_wide = data_real.astype(jnp.float32)
    imag_wide = data_imag.astype(jnp.float32)
    squares = (real_wide * real_wide + imag_wide * imag_wide).astype(jnp.bfloat16)
    inverse_count = 1.0 / (data_mass.shape[0] * event_devices)

    def field_total(coupling):
        rows = jnp.concatenate(split_two(coupling), axis=0)
        on_real = jnp.dot(rows, data_real, preferred_element_type=jnp.float32)
        on_imag = jnp.dot(rows, data_imag, preferred_element_type=jnp.float32)
        on_real = on_real[:2] + on_real[2:]
        on_imag = on_imag[:2] + on_imag[2:]
        return on_real[0] - on_imag[1], on_imag[0] + on_real[1]

    for iteration in range(ITERS):
        field_real, field_imag = field_total(coupling)
        power = field_real * field_real + field_imag * field_imag
        inverse = 1.0 / (power + BACKGROUND)
        weighting = weight_here * inverse * inverse_count
        carried = jnp.stack([field_real * weighting, field_imag * weighting])
        rows = jnp.concatenate(split_two(carried), axis=0)
        on_real = dot_last(rows, data_real)
        on_imag = dot_last(rows, data_imag)
        on_real = on_real[:2] + on_real[2:]
        on_imag = on_imag[:2] + on_imag[2:]
        bend = jnp.stack(split_two(weighting * power * inverse))
        curve = dot_last(bend, squares)
        partial = jnp.stack(
            [
                -(on_real[0] + on_imag[1]),
                -(on_real[1] - on_imag[0]),
                curve[0] + curve[1],
            ]
        )
        real_rows, imag_rows = gram[:, :waves], gram[:, waves:]
        own = jnp.stack(
            [
                jnp.sum(real_rows * coupling[0][None] - imag_rows * coupling[1][None], axis=1),
                jnp.sum(real_rows * coupling[1][None] + imag_rows * coupling[0][None], axis=1),
                jnp.sum(jnp.abs(real_rows) + jnp.abs(imag_rows), axis=1),
            ]
        )
        there = lax.dynamic_slice_in_dim(partial, gram_at, gram_rows, axis=1)
        partial = lax.dynamic_update_slice_in_dim(partial, there + own, gram_at, axis=1)
        total = jnp.sum(lax.all_gather(partial, ("event", "wrow"), axis=0), axis=0)
        coupling = coupling - total[:2] / total[2:3]
    field_real, field_imag = field_total(coupling)
    intensity = field_real * field_real + field_imag * field_imag + BACKGROUND
    intensity = lax.all_gather(intensity, "wrow", axis=0, tiled=True)
    return (lax.dynamic_slice_in_dim(coupling, mine, wave_count, axis=1), intensity)


def solution(mesh):
    placed = (
        P("event"),
        P(None, "event"),
        P("event"),
        P(None, "event"),
        P("event"),
        P("wrow"),
        P("wrow"),
        P("wrow"),
        P("wrow"),
        P(None, "wrow"),
    )
    return jax.shard_map(
        shards, mesh=mesh, in_specs=placed, out_specs=(P(None, "wrow"), P("event")), check_vma=False
    )
```

```python
import functools

import jax
import jax.numpy as jnp
from jax import lax
from jax.experimental import pallas as pl
from jax.experimental.pallas import tpu as pltpu
from jax.sharding import PartitionSpec as P

ITERS = 3
BACKGROUND = 0.5


def wave_table(res_mass, res_width, local_wave, wave_q):
    waves = jnp.arange(wave_q.shape[0], dtype=jnp.int32)[:, None]
    index = jnp.arange(res_mass.shape[0], dtype=jnp.int32)[None, :]
    mine = local_wave[None, :] == waves
    first = jnp.min(jnp.where(mine, index, res_mass.shape[0]), axis=1, keepdims=True)
    last = jnp.max(jnp.where(mine, index, -1), axis=1, keepdims=True)

    def pick(where, values):
        return jnp.sum(jnp.where(index == where, values[None, :], 0.0), axis=1)

    return jnp.stack(
        [
            pick(first, res_mass),
            pick(first, res_width),
            pick(last, res_mass),
            pick(last, res_width),
            wave_q.astype(jnp.float32),
        ]
    )


def wave_amplitudes(mass_sq, angular_basis, table):
    def shape_of(mass, width):
        product = (mass * width)[:, None]
        spacing = (mass * mass)[:, None] - mass_sq[None, :]
        scale = product / (spacing * spacing + product * product)
        return scale * spacing, scale * product

    real_a, imag_a = shape_of(table[0], table[1])
    real_b, imag_b = shape_of(table[2], table[3])
    levels = jnp.arange(angular_basis.shape[0], dtype=jnp.float32)
    chooser = (table[4][:, None] == levels[None, :]).astype(jnp.bfloat16)
    angular = jnp.dot(chooser, angular_basis, preferred_element_type=jnp.float32)
    return (
        (angular * (real_a + real_b)).astype(jnp.bfloat16),
        (angular * (imag_a + imag_b)).astype(jnp.bfloat16),
    )


def dot_last(left, right):
    return lax.dot_general(
        left, right, (((1,), (1,)), ((), ())), preferred_element_type=jnp.float32
    )


def halves(value):
    high = value.astype(jnp.bfloat16)
    return high, (value - high.astype(jnp.float32)).astype(jnp.bfloat16)


def newton_kernel(
    sizes,
    gram_ref,
    real_ref,
    imag_ref,
    squares_ref,
    weight_ref,
    start_ref,
    coupling_ref,
    intensity_ref,
    tiles,
    near,
    far,
    near_out,
    far_out,
    tile_send,
    tile_recv,
    near_send,
    near_recv,
    far_send,
    far_recv,
):
    events, rows, low = sizes
    high_count = events // low
    group = low * rows
    event = lax.axis_index("event")
    row = lax.axis_index("wrow")
    high, part = event // low, event % low
    place = part * rows + row
    me = event * rows + row
    everyone = events * rows
    mesh_id = pl.DeviceIdType.MESH

    barrier = pltpu.get_barrier_semaphore()

    def greet(step, carry):
        other = (me + step) % everyone
        pl.semaphore_signal(
            barrier, inc=1, device_id=(other // rows, other % rows), device_id_type=mesh_id
        )
        return carry

    lax.fori_loop(1, everyone, greet, 0)
    pl.semaphore_wait(barrier, everyone - 1)

    def tile_copy(step, slot):
        other = (event + step) % events
        return pltpu.make_async_remote_copy(
            src_ref=gram_ref.at[other],
            dst_ref=tiles.at[slot],
            send_sem=tile_send.at[step],
            recv_sem=tile_recv.at[slot],
            device_id=(other, row),
            device_id_type=mesh_id,
        )

    def near_copy(turn, step, slot):
        other = (place + step) % group
        return pltpu.make_async_remote_copy(
            src_ref=near_out.at[turn],
            dst_ref=near.at[turn, slot],
            send_sem=near_send.at[turn, step],
            recv_sem=near_recv.at[turn, slot],
            device_id=(high * low + other // rows, other % rows),
            device_id_type=mesh_id,
        )

    def far_copy(turn, step, slot):
        other = (high + step) % high_count
        return pltpu.make_async_remote_copy(
            src_ref=far_out.at[turn],
            dst_ref=far.at[turn, slot],
            send_sem=far_send.at[turn, step],
            recv_sem=far_recv.at[turn, slot],
            device_id=(other * low + part, row),
            device_id_type=mesh_id,
        )

    def start_all(copy, count, own):
        def body(step, carry):
            copy(step, own).start()
            return carry

        lax.fori_loop(1, count, body, 0)

    def wait_all(copy, count, own):
        def body(step, carry):
            copy(step, (own + step) % count).wait()
            return carry

        lax.fori_loop(1, count, body, 0)

    start_all(tile_copy, events, event)

    def times(values, ref):
        both = jnp.concatenate(halves(values), axis=0)
        out = jnp.dot(both, ref[...], preferred_element_type=jnp.float32)
        count = values.shape[0]
        return out[:count] + out[count:]

    def times_last(values, ref):
        both = jnp.concatenate(halves(values), axis=0)
        out = dot_last(both, ref[...])
        count = values.shape[0]
        return out[:count] + out[count:]

    def field_total(coupling):
        on_real = times(coupling, real_ref)
        on_imag = times(coupling, imag_ref)
        return on_real[0:1] - on_imag[1:2], on_imag[0:1] + on_real[1:2]

    weight = weight_ref[...]
    coupling = start_ref[...]
    waves = coupling.shape[1]
    gram_rows = gram_ref.shape[1]
    lanes = lax.broadcasted_iota(jnp.int32, (gram_rows, waves), 1)
    down = lax.broadcasted_iota(jnp.int32, (gram_rows, waves), 0)
    spot = lanes == down + (row * (gram_rows * events) + event * gram_rows)

    def placed(terms):
        column = jnp.sum(terms, axis=1, keepdims=True)
        return jnp.sum(jnp.where(spot, column, 0.0), axis=0, keepdims=True)

    real_rows = imag_rows = None
    for turn in range(ITERS):
        field_real, field_imag = field_total(coupling)
        power = field_real * field_real + field_imag * field_imag
        inverse = 1.0 / (power + BACKGROUND)
        weighting = weight * inverse
        carried = jnp.concatenate([field_real * weighting, field_imag * weighting], axis=0)
        on_real = times_last(carried, real_ref)
        on_imag = times_last(carried, imag_ref)
        curve = times_last(weighting * power * inverse, squares_ref)
        if turn == 0:
            wait_all(tile_copy, events, event)
            tiles[event] = gram_ref[event]
            gram = lax.fori_loop(
                0,
                events,
                lambda index, total: total + tiles[index].astype(jnp.float32),
                jnp.zeros((gram_rows, 2 * waves), jnp.float32),
            )
            real_rows, imag_rows = gram[:, :waves], gram[:, waves:]
        own_real = placed(real_rows * coupling[0:1] - imag_rows * coupling[1:2])
        own_imag = placed(real_rows * coupling[1:2] + imag_rows * coupling[0:1])
        own_curve = placed(jnp.abs(real_rows) + jnp.abs(imag_rows))
        partial = jnp.concatenate(
            [
                own_real - (on_real[0:1] + on_imag[1:2]),
                own_imag - (on_real[1:2] - on_imag[0:1]),
                own_curve + curve,
                jnp.zeros((1, waves), jnp.float32),
            ],
            axis=0,
        )
        near_out[turn] = partial
        near[turn, place] = partial
        start_all(functools.partial(near_copy, turn), group, place)
        wait_all(functools.partial(near_copy, turn), group, place)
        total = near[turn, 0]
        for slot in range(1, group):
            total = total + near[turn, slot]
        far_out[turn] = total
        far[turn, high] = total
        start_all(functools.partial(far_copy, turn), high_count, high)
        wait_all(functools.partial(far_copy, turn), high_count, high)
        total = far[turn, 0]
        for slot in range(1, high_count):
            total = total + far[turn, slot]
        coupling = coupling - total[0:2] / total[2:3]
    coupling_ref[...] = coupling
    field_real, field_imag = field_total(coupling)
    intensity_ref[...] = field_real * field_real + field_imag * field_imag + BACKGROUND


def newton(gram_blocks, data_real, data_imag, squares, weight, coupling, rows):
    events, gram_rows, twice = gram_blocks.shape
    waves, share = data_real.shape
    low = max(size for size in range(1, events + 1) if events % size == 0 and size * size <= events)
    group, high = low * rows, events // low
    dma = pltpu.SemaphoreType.DMA
    return pl.pallas_call(
        functools.partial(newton_kernel, (events, rows, low)),
        out_shape=(
            jax.ShapeDtypeStruct((2, waves), jnp.float32),
            jax.ShapeDtypeStruct((1, share), jnp.float32),
        ),
        in_specs=[pl.BlockSpec(memory_space=pltpu.VMEM)] * 6,
        out_specs=(pl.BlockSpec(memory_space=pltpu.VMEM),) * 2,
        scratch_shapes=[
            pltpu.VMEM((events, gram_rows, twice), jnp.bfloat16),
            pltpu.VMEM((ITERS, group, 4, waves), jnp.float32),
            pltpu.VMEM((ITERS, high, 4, waves), jnp.float32),
            pltpu.VMEM((ITERS, 4, waves), jnp.float32),
            pltpu.VMEM((ITERS, 4, waves), jnp.float32),
            dma((events,)),
            dma((events,)),
            dma((ITERS, group)),
            dma((ITERS, group)),
            dma((ITERS, high)),
            dma((ITERS, high)),
        ],
        compiler_params=pltpu.CompilerParams(
            collective_id=0, has_side_effects=True, vmem_limit_bytes=40 * 1024 * 1024
        ),
    )(gram_blocks, data_real, data_imag, squares, weight, coupling)


def shards(
    mc_mass,
    mc_basis,
    data_mass,
    data_basis,
    data_weight,
    res_mass,
    res_width,
    res_wave,
    wave_q,
    couplings,
):
    wave_count = wave_q.shape[0]
    event_devices = lax.axis_size("event")
    row_devices = lax.axis_size("wrow")
    row_index = lax.axis_index("wrow")
    local = wave_table(res_mass, res_width, res_wave - row_index * wave_count, wave_q)
    gathered = lax.all_gather(
        jnp.concatenate([local, couplings], axis=0), "wrow", axis=1, tiled=True
    )
    table, coupling = gathered[:5], gathered[5:7]
    waves = gathered.shape[1]
    mine = row_index * wave_count

    mc_real, mc_imag = wave_amplitudes(mc_mass, mc_basis, table)
    left = jnp.concatenate(
        [
            lax.dynamic_slice_in_dim(mc_real, mine, wave_count),
            lax.dynamic_slice_in_dim(mc_imag, mine, wave_count),
        ],
        axis=0,
    )
    by_real = dot_last(left, mc_real)
    by_imag = dot_last(left, mc_imag)
    normalize = 1.0 / (mc_mass.shape[0] * event_devices)
    gram_part = jnp.concatenate(
        [
            (by_real[:wave_count] + by_imag[wave_count:]) * normalize,
            (by_imag[:wave_count] - by_real[wave_count:]) * normalize,
        ],
        axis=1,
    )
    gram_blocks = gram_part.astype(jnp.bfloat16).reshape(
        event_devices, wave_count // event_devices, 2 * waves
    )

    share = data_mass.shape[0] // row_devices
    start = row_index * share
    mass_here = lax.dynamic_slice_in_dim(data_mass, start, share)
    basis_here = lax.dynamic_slice_in_dim(data_basis, start, share, axis=1)
    weight_here = lax.dynamic_slice_in_dim(data_weight, start, share)
    data_real, data_imag = wave_amplitudes(mass_here, basis_here, table)
    real_wide = data_real.astype(jnp.float32)
    imag_wide = data_imag.astype(jnp.float32)
    squares = (real_wide * real_wide + imag_wide * imag_wide).astype(jnp.bfloat16)
    inverse_count = 1.0 / (data_mass.shape[0] * event_devices)

    coupling, intensity = newton(
        gram_blocks,
        data_real,
        data_imag,
        squares,
        (weight_here * inverse_count)[None],
        coupling,
        row_devices,
    )
    intensity = intensity[0]
    intensity = lax.all_gather(intensity, "wrow", axis=0, tiled=True)
    return (lax.dynamic_slice_in_dim(coupling, mine, wave_count, axis=1), intensity)


def solution(mesh):
    placed = (
        P("event"),
        P(None, "event"),
        P("event"),
        P(None, "event"),
        P("event"),
        P("wrow"),
        P("wrow"),
        P("wrow"),
        P("wrow"),
        P(None, "wrow"),
    )
    return jax.shard_map(
        shards, mesh=mesh, in_specs=placed, out_specs=(P(None, "wrow"), P("event")), check_vma=False
    )
```
